128 devices in a mesh: dp: 8 (over x, core), cent: 16 (over y, z).
Axes of the slice: x: 4, y: 4, z: 4, core: 2. Of those that a mesh axis runs over, the one named last changes fastest.
Arguments:
- vectors: bfloat16 [32768, 256], P(('dp', 'cent')), may hold values from -64 to 64
- owners: int32 [32768, 8], P(('dp', 'cent')), may hold values from 0 to 127, all different within a row; in each aligned block of 256 rows (0 to 255, 256 to 511, ...) at most 32 rows name the same one
- centroids: bfloat16 [262144, 256], P(('dp', 'cent')), may hold values from -6 to 6
- penalty: int32 [262144], P(('dp', 'cent')), may hold values from 0 to 7
Outputs:
- refined: float32 [262144, 256], P(('dp', 'cent'))
- energy: float32 [], replicated
The draws below stay inside these ranges and needn't reach their ends.
Inputs may be any that keep to these rules, and one draw needn't show every extreme that they name: `owners`: each row names 8 different partitions; within the rows of one device no partition is named more than 32 times, a bound that some block reaches.
All inputs are finite; a program needn't handle non-finite values.
Results may differ from the reference program's by a relative error of at most 0.003.
Values may be sent and summed in bfloat16 or wider, within the bound.
A program may use at most 64 MiB of HBM per device.

```python
import math
import jax
import jax.numpy as jnp
import numpy as np
from jax import lax

D = 256
K = 262144
VEC_DEV = 256
REPL = 8
NVEC = 32768
KLOC = 2048
CAP = 32
N_DP = 8
N_CENT = 16


def draw_vectors(key, part):
    key = jax.random.fold_in(key, 11)
    noise_key = jax.random.fold_in(key, 0)
    base = jnp.clip(jax.random.normal(noise_key, (NVEC, D), jnp.float32), -4.5, 4.5)
    row_scale = jnp.sqrt(1.0 + 4.0 * jnp.arange(NVEC, dtype=jnp.float32) / (NVEC - 1))
    return (base * row_scale[:, None]).astype(jnp.bfloat16)


def plant(result, rng, least, high):
    shape = result.shape
    place = [jax.random.randint(jax.random.fold_in(rng, axis), (), 0, shape[axis]) for axis in range(len(shape))]
    result = result.at[tuple(place)].set(least)
    longest = shape.index(max(shape))
    place[longest] = (place[longest] + 1) % shape[longest]
    return result.at[tuple(place)].set(high)


def levels(stream_key, shape, cuts, least, largest):
    loudness, own = 1.0, jax.random.fold_in(stream_key, 6)
    for position, blocks in cuts:
        steps = jnp.exp(jax.random.uniform(jax.random.fold_in(own, position), (blocks,), jnp.float32, least / len(cuts), largest / len(cuts)))
        loudness = loudness * jnp.repeat(steps, shape[position] // blocks).reshape([-1 if axis == position else 1 for axis in range(len(shape))])
    return loudness


def shared_out(key, own, number, rows, count, top, reach, slope):
    ranking = jax.random.permutation(key, count)
    heavy_load, usual = shares(count, rows * top, reach, slope, True), shares(count, rows * top, reach, slope, False)
    places = jnp.arange(count)

    def named(lengths, turn):
        used = int((lengths > 0).sum())
        fixed = max(1, used // 4)
        shifted = fixed + (places - fixed + turn * (used - fixed)) % max(1, count - fixed)
        return jnp.zeros((count,), jnp.int32).at[ranking[jnp.where(places < fixed, places, shifted)]].set(jnp.asarray(lengths, jnp.int32))

    lengths = jnp.where(number % 4 == 0, named(heavy_load, number // 4), named(usual, number - number // 4 - 1))
    mixed = jax.random.permutation(jax.random.fold_in(own, 3), count)
    donor, sink = mixed[0:count // 2 * 2:2], mixed[1:count // 2 * 2:2]
    slack = jnp.minimum(lengths[donor] - 1, reach - lengths[sink]) // 2
    slack = jnp.where((donor == ranking[0]) | (sink == ranking[0]) | (lengths[sink] == 0), 0, jnp.maximum(slack, 0))
    shifted = jax.random.randint(jax.random.fold_in(own, 4), (count // 2,), 0, 1 << 20) % (slack + 1)
    lengths = lengths.at[donor].add(-shifted).at[sink].add(shifted)
    labels = jnp.searchsorted(jnp.cumsum(lengths), jnp.arange(rows * top), side="right").astype(jnp.int32)
    listing = labels.reshape(top, rows).T
    listing = listing[jax.random.permutation(jax.random.fold_in(own, 1), rows)]
    turn = jax.random.randint(jax.random.fold_in(own, 2), (rows, 1), 0, top)
    return jnp.take_along_axis(listing, (jnp.arange(top)[None, :] + turn) % top, axis=1)


def shares(number_of, total, bound, slope, full):
    weights = [(1 << 20) // math.isqrt(rank ** slope) + 1 for rank in range(1, number_of + 1)]
    largest = bound if full else min(bound, max(-(-total // number_of), total * weights[0] // sum(weights)))
    least = 1 if total - largest >= number_of - 1 else 0
    given, surplus = [largest] + [least] * (number_of - 1), total - largest - least * (number_of - 1)
    while surplus > 0:
        movable = [i for i in range(1, number_of) if given[i] < largest] or [i for i in range(1, number_of) if given[i] < bound]
        pool, left = sum([weights[i] for i in movable]), surplus
        for i in movable:
            more = min(bound - given[i], max(1, left * weights[i] // pool), surplus)
            given[i] = given[i] + more
            surplus = surplus - more
    return np.array(given)


def gaussian(stream_key, extent, spread, limit, pieces=(), held_as=jnp.bfloat16):
    values = jax.random.normal(stream_key, extent, jnp.float32) * spread
    if len(pieces) > 0:
        values = levels(stream_key, extent, pieces, -0.22, 0.18) * values
    return jnp.clip(values, min=-limit, max=limit).astype(held_as)


def setup_inputs(seed: int = 0) -> dict:
    key_of = jax.random.split(jax.random.key(seed), 5)
    vectors = draw_vectors(jax.random.fold_in(key_of[4], 71), 0)
    owners_keys = jax.random.split(jax.random.fold_in(key_of[1], 1), NVEC // VEC_DEV)
    owners_turns = jax.random.permutation(jax.random.fold_in(key_of[1], 3), NVEC // VEC_DEV)
    owners = jax.vmap(lambda own, number: shared_out(jax.random.fold_in(key_of[1], 2), own, number, VEC_DEV, N_DP * N_CENT, REPL, CAP, 2))(owners_keys, owners_turns).reshape((NVEC, REPL))
    centroids = gaussian(key_of[2], (K, D), 1.0, 6.0, ((0, 128),))
    penalty = plant(jax.random.randint(key_of[3], (K,), 0, 8), jax.random.fold_in(key_of[3], 1), 0, 7).astype(jnp.int32)
    return dict(vectors=vectors, owners=owners, centroids=centroids, penalty=penalty)


sharpness = 4.0
penalty_weight = 0.5
energy_scale = 16.0


def reference(vectors, owners, centroids, penalty):
    partitions = N_DP * N_CENT
    max_rows = partitions * CAP
    slot_count = NVEC * REPL
    feats = vectors.astype(jnp.float32)
    mean_sq = jnp.sum(feats * feats) / (NVEC * D)
    score_scale = 1.0 / (sharpness * mean_sq)
    targets = owners.reshape(-1).astype(jnp.int32)
    order = jnp.argsort(targets, stable=True).astype(jnp.int32)
    counts = jax.ops.segment_sum(jnp.ones_like(targets), targets, num_segments=partitions).astype(jnp.int32)
    starts = (jnp.cumsum(counts) - counts).astype(jnp.int32)
    padded_order = jnp.concatenate([order, jnp.zeros((max_rows,), jnp.int32)])
    cent_all = centroids.astype(jnp.float32).reshape(partitions, KLOC, D)
    offsets = (penalty_weight * penalty.astype(jnp.float32)).reshape(partitions, KLOC)

    def gather_rows(index):
        slots = lax.dynamic_slice_in_dim(padded_order, starts[index], max_rows)
        valid = jnp.arange(max_rows, dtype=jnp.int32) < counts[index]
        return slots, valid, feats[slots // REPL]

    def logits_for(index, row_block):
        cent = cent_all[index]
        inner = jnp.dot(row_block, cent.T, precision=lax.Precision.HIGHEST)
        row_norms = jnp.sum(row_block * row_block, axis=1)
        cent_norms = jnp.sum(cent * cent, axis=1)
        return -(row_norms[:, None] - 2.0 * inner + cent_norms[None, :]) * score_scale - offsets[index][None, :]

    def first_pass(index):
        slots, valid, row_block = gather_rows(index)
        logits = logits_for(index, row_block)
        peak_val = jnp.max(logits, axis=1)
        totals = jnp.sum(jnp.exp(logits - peak_val[:, None]), axis=1)
        return jnp.where(valid, slots, slot_count), peak_val, totals

    part_ids = jnp.arange(partitions, dtype=jnp.int32)
    placed, peaks, totals = lax.map(first_pass, part_ids)
    placed = placed.reshape(-1)
    slot_peak = jnp.zeros((slot_count,), jnp.float32).at[placed].set(peaks.reshape(-1), mode="drop")
    slot_total = jnp.zeros((slot_count,), jnp.float32).at[placed].set(totals.reshape(-1), mode="drop")
    slot_peak = slot_peak.reshape(NVEC, REPL)
    slot_total = slot_total.reshape(NVEC, REPL)
    row_peak = jnp.max(slot_peak, axis=1)
    log_norm = row_peak + jnp.log(jnp.sum(slot_total * jnp.exp(slot_peak - row_peak[:, None]), axis=1))
    slot_norm = jnp.repeat(log_norm, REPL)

    def second_pass(index):
        slots, valid, row_block = gather_rows(index)
        logits = logits_for(index, row_block)
        norm_rows = slot_norm[slots]
        weights = (jnp.exp(logits - norm_rows[:, None]) * valid.astype(jnp.float32)[:, None]).astype(jnp.bfloat16).astype(jnp.float32)
        numerator = jnp.dot(weights.T, row_block, precision=lax.Precision.HIGHEST)
        weight_sum = jnp.sum(weights, axis=0)
        return (cent_all[index] + numerator) / (1.0 + weight_sum[:, None])

    refined = lax.map(second_pass, part_ids).reshape(K, D)
    energy = -jnp.sum(log_norm) / (energy_scale * NVEC)
    return refined, energy
```

```python
import math

import jax
import jax.numpy as jnp
from jax import lax
from jax.experimental import pallas as pl
from jax.experimental.pallas import tpu as pltpu
from jax.sharding import PartitionSpec as P

sharpness = 4.0
penalty_weight = 0.5
energy_scale = 16.0

AXES = ("dp", "cent")
CAP = 32
DEAD = 3.0e38
LOG2E = math.log2(math.e)
LN2 = math.log(2.0)
MIB = 1024 * 1024

f32 = jnp.float32
bf16 = jnp.bfloat16
i32 = jnp.int32


def nt(a, b):
    return lax.dot_general(a, b, (((1,), (1,)), ((), ())), preferred_element_type=f32)


def iota(shape, axis):
    return lax.broadcasted_iota(i32, shape, axis)


def arrange(quarter, owners_t, vectors_ref, out_ref, rank_ref, src_ref):
    rows = vectors_ref.shape[0]
    parts = rank_ref.shape[0]
    part = iota((parts, rows), 0)
    match = part == owners_t[0:1, :]
    for r in range(1, owners_t.shape[0]):
        match = match | (part == owners_t[r : r + 1, :])
    before = jnp.where(iota((rows, rows), 0) < iota((rows, rows), 1), 1.0, 0.0).astype(bf16)
    rank = jnp.dot(jnp.where(match, 1.0, 0.0).astype(bf16), before, preferred_element_type=f32)
    rank_ref[...] = jnp.where(match, rank.astype(i32), -1)
    step = 8
    for g in range(parts // step):
        ranks = rank_ref[g * step : (g + 1) * step, :]
        hot = ranks[:, None, :] == iota((step, CAP, rows), 1)
        hot = jnp.where(hot, 1.0, 0.0).astype(bf16).reshape(step * CAP, rows)
        picked = jnp.dot(hot, vectors_ref[...], preferred_element_type=f32)
        out_ref[g * step * CAP : (g + 1) * step * CAP, :] = picked.astype(bf16)
    ranks = rank_ref[...]
    row = iota((parts, rows), 1)
    lane = iota((parts, 128), 1)
    src = jnp.full((parts, 128), -1, i32)
    for j in range(CAP):
        here = jnp.max(jnp.where(ranks == j, row, -1), axis=1, keepdims=True)
        src = jnp.where(lane == quarter * CAP + j, here, src)
    src_ref[...] = src


def fill_bias(mean_sq, centroids_ref, penalty_ref, bias_ref):
    n = centroids_ref.shape[0]
    eye = iota((128, 128), 0) == iota((128, 128), 1)
    for g in range(n // 128):
        c = centroids_ref[g * 128 : (g + 1) * 128, :].astype(f32)
        c = c * c
        half = sum(c[:, i : i + 128] for i in range(0, c.shape[1], 128)) * 0.5
        pen = penalty_ref[g : g + 1, :].astype(f32) * (penalty_weight * sharpness * 0.5 * mean_sq)
        col = jnp.sum(half + jnp.where(eye, pen, 0.0), axis=1, keepdims=True)
        bias_ref[g * 128 : (g + 1) * 128, :] = jnp.broadcast_to(col, (128, 128))


def wide(ref, rows, width):
    b = ref[rows, :]
    return jnp.concatenate([b] * (width // 128), axis=1)


def chunk_stats(factor, x, centroids_ref, bias_ref, u_ref, kb):
    n = centroids_ref.shape[0]
    width = x.shape[0]
    peak = jnp.full((8, width), -DEAD, f32)
    for k in range(0, n, kb):
        u = nt(centroids_ref[k : k + kb, :], x) - wide(bias_ref, pl.ds(k, kb), width)
        u_ref[k : k + kb, :] = u
        peak = jnp.maximum(peak, jnp.max(u.reshape(kb // 8, 8, width), axis=0))
    peak = jnp.max(peak, axis=0, keepdims=True)
    total = jnp.zeros((8, width), f32)
    for k in range(0, n, kb):
        p = jnp.exp2((u_ref[k : k + kb, :] - peak) * factor)
        total = total + jnp.sum(p.reshape(kb // 8, 8, width), axis=0)
    return peak * factor + jnp.log2(jnp.sum(total, axis=0, keepdims=True))


def home(quarter, scale, local_sq, lse, ranks_ref, src_ref):
    parts, rows = ranks_ref.shape
    logs = []
    for h in range(0, rows, 128):
        ranks = ranks_ref[:, h : h + 128]
        got = jnp.take_along_axis(lse, jnp.maximum(ranks, 0) + quarter * CAP, axis=1)
        got = jnp.where(ranks >= 0, got, -DEAD)
        peak = jnp.max(got, axis=0, keepdims=True)
        total = jnp.sum(jnp.where(ranks >= 0, jnp.exp2(got - peak), 0.0), axis=0, keepdims=True)
        logs.append(peak + jnp.log2(total))
    src = src_ref[...]
    norm = jnp.full((parts, 128), DEAD, f32)
    for h, log in enumerate(logs):
        got = jnp.take_along_axis(jnp.broadcast_to(log, (parts, 128)), jnp.bitwise_and(src, 127), axis=1)
        norm = jnp.where((src >= h * 128) & (src < (h + 1) * 128), got, norm)
    log_sum = LN2 * jnp.sum(sum(logs), axis=1, keepdims=True) - scale * local_sq
    spare = lax.rem(quarter + 1, 4) * CAP
    return jnp.where(iota((parts, 128), 1) == spare, log_sum, norm)


def arrange_kernel(owners_ref, vectors_ref, out_ref, rank_ref, src_ref):
    quarter = lax.rem(lax.axis_index("cent"), 4)
    arrange(quarter, owners_ref[...].T, vectors_ref, out_ref, rank_ref, src_ref)


def stats_kernel(mean_ref, x_ref, centroids_ref, penalty_ref, lse_ref, bias_ref, u_ref):
    mean_sq = mean_ref[0, 0]
    factor = LOG2E * 2.0 / (sharpness * mean_ref[0:1, :])
    factor = jnp.concatenate([factor, factor], axis=1)
    fill_bias(mean_sq, centroids_ref, penalty_ref, bias_ref)

    def chunk(t, _):
        x = x_ref[pl.ds(pl.multiple_of(t * 256, 256), 256), :]
        lse = chunk_stats(factor, x, centroids_ref, bias_ref, u_ref, 256)
        for half in range(2):
            row = lse[:, half * 128 : (half + 1) * 128]
            lse_ref[pl.ds(pl.multiple_of(t * 8 + half * 4, 4), 4)] = jnp.broadcast_to(row, (4, 1, 128))
        return 0

    lax.fori_loop(0, x_ref.shape[0] // 256, chunk, 0)


def home_kernel(mean_ref, sq_ref, lse_ref, rank_ref, src_ref, norm_ref):
    quarter = lax.rem(lax.axis_index("cent"), 4)
    lse = lse_ref[...].reshape(rank_ref.shape[0], 128)
    scale = 1.0 / (sharpness * mean_ref[0:1, 0:1])
    norm = home(quarter, scale, sq_ref[0:1, 0:1], lse, rank_ref, src_ref)
    norm_ref[...] = norm.reshape(norm_ref.shape)


def unpack_norms(norm, norm_ref):
    parts = norm.shape[0]
    lane = iota((parts, 128), 1)
    row = iota((parts, 128), 0)
    spare = lax.rem(lax.rem(row, 4) + 1, 4) * CAP
    log_sum = jnp.sum(jnp.where(lane == spare, norm, 0.0))
    mine = jnp.where(lane // CAP == lax.rem(row, 4), norm, 0.0)
    norm_ref[...] = jnp.sum(mine.reshape(parts // 4, 4, 128), axis=1)[:, None, :]
    return log_sum


def final_kernel(mean_ref, norm_in_ref, x_ref, centroids_ref, penalty_ref, out_ref, energy_ref, bias_ref, norm_ref):
    parts = norm_in_ref.shape[0]
    mean_sq = mean_ref[0, 0]
    factor = LOG2E * 2.0 / (sharpness * mean_ref[0:1, :])
    factor = jnp.concatenate([factor, factor], axis=1)
    fill_bias(mean_sq, centroids_ref, penalty_ref, bias_ref)
    log_sum = unpack_norms(norm_in_ref[...].reshape(parts, 128), norm_ref)
    energy_ref[...] = jnp.full(energy_ref.shape, -log_sum / (energy_scale * x_ref.shape[0] / CAP * 256), f32)
    slots = x_ref.shape[0]
    n, d = centroids_ref.shape
    kb = 256

    def block(b, _):
        rows = pl.ds(pl.multiple_of(b * kb, kb), kb)
        c = centroids_ref[rows, :]
        bias = wide(bias_ref, rows, 256)
        acc = jnp.zeros((kb, d), f32)
        mass = jnp.zeros((kb, 128), f32)
        for t in range(slots // 256):
            x = x_ref[t * 256 : (t + 1) * 256, :]
            norm = jnp.concatenate([norm_ref[2 * t], norm_ref[2 * t + 1]], axis=1)
            w = jnp.exp2((nt(c, x) - bias) * factor - norm).astype(bf16)
            acc = acc + jnp.dot(w, x, preferred_element_type=f32)
            w = w.astype(f32)
            mass = mass + w[:, :128] + w[:, 128:]
        mass = jnp.sum(mass, axis=1, keepdims=True)
        out_ref[rows, :] = (c.astype(f32) + acc) / (1.0 + mass)
        return 0

    lax.fori_loop(0, n // kb, block, 0)


def call(kernel, out_shape, scratch, *args):
    return pl.pallas_call(
        kernel,
        out_shape=out_shape,
        scratch_shapes=scratch,
        compiler_params=pltpu.CompilerParams(vmem_limit_bytes=56 * MIB),
    )(*args)


def exchange(x):
    return lax.all_to_all(x, AXES, split_axis=0, concat_axis=0, tiled=True)


def body(vectors, owners, centroids, penalty):
    rows, d = vectors.shape
    parts = lax.axis_size(AXES)
    n = centroids.shape[0]
    slots = parts * CAP
    shape = jax.ShapeDtypeStruct
    local_sq = jnp.sum(jnp.square(vectors.astype(f32)))
    all_sq = exchange(jnp.broadcast_to(local_sq, (parts, 1, 128)))
    mean_sq = jnp.sum(all_sq, axis=0) / (rows * parts * d)
    sq = jnp.broadcast_to(local_sq, (1, 128))
    penalty = penalty.reshape(n // 128, 128)
    out, rank, src = call(
        arrange_kernel,
        (shape((slots, d), bf16), shape((parts, rows), i32), shape((parts, 128), i32)),
        [],
        owners,
        vectors,
    )
    x = exchange(out.reshape(parts, CAP, d)).reshape(slots, d)
    lse = call(
        stats_kernel,
        shape((parts, 1, 128), f32),
        [pltpu.VMEM((n, 128), f32), pltpu.VMEM((n, 256), f32)],
        mean_sq,
        x,
        centroids,
        penalty,
    )
    norm = call(home_kernel, shape((parts, 1, 128), f32), [], mean_sq, sq, exchange(lse), rank, src)
    refined, energy = call(
        final_kernel,
        (shape((n, d), f32), shape((1, 128), f32)),
        [pltpu.VMEM((n, 128), f32), pltpu.VMEM((slots // 128, 1, 128), f32)],
        mean_sq,
        exchange(norm),
        x,
        centroids,
        penalty,
    )
    return refined, energy[0, 0]


def solution(mesh):
    placed = (P(AXES, None), P(AXES, None), P(AXES, None), P(AXES))
    return jax.shard_map(
        body, mesh=mesh, in_specs=placed, out_specs=(P(AXES, None), P()), check_vma=False
    )
```

```python
import math

import jax
import jax.numpy as jnp
from jax import lax
from jax.experimental import pallas as pl
from jax.experimental.pallas import tpu as pltpu
from jax.sharding import PartitionSpec as P

sharpness = 4.0
penalty_weight = 0.5
energy_scale = 16.0

AXES = ("dp", "cent")
CAP = 32
DEAD = 3.0e38
LOG2E = math.log2(math.e)
LN2 = math.log(2.0)
MIB = 1024 * 1024

f32 = jnp.float32
bf16 = jnp.bfloat16
i32 = jnp.int32


def nt(a, b):
    return lax.dot_general(a, b, (((1,), (1,)), ((), ())), preferred_element_type=f32)


def iota(shape, axis):
    return lax.broadcasted_iota(i32, shape, axis)


PARTS = 128
INNER = 16
OUTER = 8
STRIDE = 37
GROUP = 8
LOGICAL = pl.DeviceIdType.LOGICAL


def jump(i):
    return lax.rem(i * STRIDE, PARTS)


def ahead(dp, cent, i):
    j = jump(i)
    return lax.rem(dp + j // INNER, OUTER) * INNER + lax.rem(cent + lax.rem(j, INNER), INNER)


def behind(dp, cent, i):
    j = jump(i)
    return lax.rem(dp + OUTER - j // INNER, OUTER) * INNER + lax.rem(cent + INNER - lax.rem(j, INNER), INNER)


def arrange(dp, cent, owners_t, vectors_ref, out_ref, rank_ref, src_ref):
    rows = vectors_ref.shape[0]
    step = iota((PARTS, rows), 0)
    j = jnp.bitwise_and(step * STRIDE, PARTS - 1)
    outer = jnp.bitwise_and(dp + jnp.right_shift(j, 4), OUTER - 1)
    part = outer * INNER + jnp.bitwise_and(cent + j, INNER - 1)
    match = part == owners_t[0:1, :]
    for r in range(1, owners_t.shape[0]):
        match = match | (part == owners_t[r : r + 1, :])
    before = jnp.where(iota((rows, rows), 0) < iota((rows, rows), 1), 1.0, 0.0).astype(bf16)
    rank = jnp.dot(jnp.where(match, 1.0, 0.0).astype(bf16), before, preferred_element_type=f32)
    rank_ref[...] = jnp.where(match, rank.astype(i32), -1)
    for g in range(PARTS // GROUP):
        ranks = rank_ref[g * GROUP : (g + 1) * GROUP, :]
        hot = ranks[:, None, :] == iota((GROUP, CAP, rows), 1)
        hot = jnp.where(hot, 1.0, 0.0).astype(bf16).reshape(GROUP * CAP, rows)
        picked = jnp.dot(hot, vectors_ref[...], preferred_element_type=f32).astype(bf16)
        out_ref[g * GROUP : (g + 1) * GROUP] = picked.reshape(GROUP, CAP, picked.shape[1])


def invert_ranks(rank_ref, src_ref):
    rows = rank_ref.shape[1]
    ranks = rank_ref[...]
    row = iota((PARTS, rows), 1)
    slot = iota((PARTS, 128), 1) - jnp.bitwise_and(iota((PARTS, 128), 0), 3) * CAP
    src = jnp.full((PARTS, 128), -1, i32)
    for j in range(CAP):
        here = jnp.max(jnp.where(ranks == j, row, -1), axis=1, keepdims=True)
        src = jnp.where(slot == j, here, src)
    src_ref[...] = src


def fill_bias(mean, centroids_ref, penalty_ref, bias_ref):
    n = centroids_ref.shape[0]
    eye = iota((128, 128), 0) == iota((128, 128), 1)
    for g in range(n // 128):
        c = centroids_ref[g * 128 : (g + 1) * 128, :].astype(f32)
        c = c * c
        half = sum(c[:, i : i + 128] for i in range(0, c.shape[1], 128)) * 0.5
        pen = penalty_ref[g : g + 1, :].astype(f32) * (penalty_weight * sharpness * 0.5) * mean
        col = jnp.sum(half + jnp.where(eye, pen, 0.0), axis=1, keepdims=True)
        bias_ref[g * 128 : (g + 1) * 128, :] = jnp.broadcast_to(col, (128, 128))


def chunk_stats(factor, x, t, centroids_ref, bias_ref, u_ref, kb):
    n = centroids_ref.shape[0]
    width = x.shape[0]
    peak = jnp.full((8, width), -DEAD, f32)
    for k in range(0, n, kb):
        b = bias_ref[k : k + kb, :]
        u = nt(centroids_ref[k : k + kb, :], x) - jnp.concatenate([b, b], axis=1)
        u_ref[t, k : k + kb, :] = u
        peak = jnp.maximum(peak, jnp.max(u.reshape(kb // 8, 8, width), axis=0))
    peak = jnp.max(peak, axis=0, keepdims=True)
    total = jnp.zeros((8, width), f32)
    for k in range(0, n, kb):
        p = jnp.exp2((u_ref[t, k : k + kb, :] - peak) * factor)
        total = total + jnp.sum(p.reshape(kb // 8, 8, width), axis=0)
    return peak * factor + jnp.log2(jnp.sum(total, axis=0, keepdims=True))


def home(mean, local_sq, lse, rank_ref, src_ref):
    rows = rank_ref.shape[1]
    quarter = jnp.bitwise_and(iota((PARTS, 128), 0), 3) * CAP
    logs = []
    for h in range(0, rows, 128):
        ranks = rank_ref[:, h : h + 128]
        live = ranks >= 0
        got = jnp.take_along_axis(lse, jnp.maximum(ranks, 0) + quarter, axis=1)
        peak = jnp.max(jnp.where(live, got, -DEAD), axis=0, keepdims=True)
        total = jnp.sum(jnp.where(live, jnp.exp2(got - peak), 0.0), axis=0, keepdims=True)
        logs.append(peak + jnp.log2(total))
    src = src_ref[...]
    norm = jnp.full((PARTS, 128), DEAD, f32)
    for h, log in enumerate(logs):
        got = jnp.take_along_axis(jnp.broadcast_to(log, (PARTS, 128)), jnp.bitwise_and(src, 127), axis=1)
        norm = jnp.where((src >= h * 128) & (src < (h + 1) * 128), got, norm)
    log_sum = LN2 * jnp.sum(sum(logs), axis=1, keepdims=True) - local_sq / (sharpness * mean)
    spare = jnp.bitwise_and(quarter + CAP, 127)
    return jnp.where(iota((PARTS, 128), 1) == spare, log_sum, norm)


def unpack_norms(dp, cent, norm, norm_ref):
    lane = iota((PARTS, 128), 1)
    j = jnp.bitwise_and(iota((PARTS, 128), 0) * STRIDE, PARTS - 1)
    outer = jnp.bitwise_and(dp + OUTER - jnp.right_shift(j, 4), OUTER - 1)
    sender = outer * INNER + jnp.bitwise_and(cent + PARTS - j, INNER - 1)
    quarter = jnp.bitwise_and(iota((PARTS, 128), 0), 3) * CAP
    spare = jnp.bitwise_and(quarter + CAP, 127)
    log_sum = jnp.sum(jnp.where(lane == spare, norm, 0.0), axis=1, keepdims=True)
    log_sum = jnp.sum(jnp.where(lane == sender, log_sum, 0.0), axis=0, keepdims=True)
    log_sum = jnp.sum(log_sum, axis=1, keepdims=True)
    mine = jnp.where(jnp.bitwise_and(lane, 96) == quarter, norm, 0.0)
    norm_ref[...] = jnp.sum(mine.reshape(PARTS // 4, 4, 128), axis=1)
    return log_sum


def kernel(
    owners_ref, vectors_ref, centroids_ref, penalty_ref, out_ref, energy_ref,
    send_ref, x_ref, u_ref, bias_ref, rank_ref, src_ref,
    sq_ref, outer_ref, inner_ref, lse_ref, lse_in_ref, norm_ref, norm_in_ref, norms_ref,
    x_out, x_in, sq_out, sq_in, lse_out, lse_in, norm_out, norm_in,
):
    dp, cent = lax.axis_index("dp"), lax.axis_index("cent")
    n, d = centroids_ref.shape
    rows = vectors_ref.shape[0]
    barrier = pltpu.get_barrier_semaphore()

    def greet(i, _):
        pl.semaphore_signal(barrier, inc=1, device_id=ahead(dp, cent, i), device_id_type=LOGICAL)
        return 0

    lax.fori_loop(1, PARTS, greet, 0)
    arrange(dp, cent, owners_ref[...].T, vectors_ref, send_ref, rank_ref, src_ref)
    x_ref[0] = send_ref[0]
    v = vectors_ref[...].astype(f32)
    local_sq = jnp.sum(jnp.sum(v * v, axis=0, keepdims=True), axis=1, keepdims=True)
    sq_ref[0] = jnp.broadcast_to(local_sq, (1, 128))
    outer_ref[0] = sq_ref[0]
    pl.semaphore_wait(barrier, PARTS - 1)

    def copy(src, dst, out_sem, in_sem, device):
        return pltpu.make_async_remote_copy(
            src_ref=src, dst_ref=dst, send_sem=out_sem, recv_sem=in_sem, device_id=device, device_id_type=LOGICAL
        )

    def wait_bytes(ref, sem):
        pltpu.make_async_copy(ref, ref, sem).wait()

    for i in range(1, OUTER):
        device = lax.rem(dp + i, OUTER) * INNER + cent
        copy(sq_ref.at[0], outer_ref.at[i], sq_out.at[0], sq_in.at[0], device).start()

    def send(i, _):
        copy(send_ref.at[i], x_ref.at[i], x_out, x_in.at[i // GROUP], ahead(dp, cent, i)).start()
        return 0

    lax.fori_loop(1, PARTS, send, 0)
    wait_bytes(outer_ref.at[pl.ds(1, OUTER - 1)], sq_in.at[0])
    sq_ref[1] = jnp.sum(outer_ref[...], axis=0)
    inner_ref[0] = sq_ref[1]
    for i in range(1, INNER):
        device = dp * INNER + lax.rem(cent + i, INNER)
        copy(sq_ref.at[1], inner_ref.at[i], sq_out.at[1], sq_in.at[1], device).start()
    invert_ranks(rank_ref, src_ref)
    wait_bytes(inner_ref.at[pl.ds(1, INNER - 1)], sq_in.at[1])
    mean = jnp.sum(inner_ref[...], axis=0) * (1.0 / (rows * PARTS * d))
    fill_bias(mean, centroids_ref, penalty_ref, bias_ref)
    factor = LOG2E * 2.0 / (sharpness * mean)
    factor = jnp.concatenate([factor, factor], axis=1)

    def send_lse(i, _):
        copy(lse_ref.at[i // 4], lse_in_ref.at[i], lse_out, lse_in, behind(dp, cent, i)).start()
        return 0

    def chunk(t):
        x = x_ref[pl.ds(t * GROUP, GROUP)].reshape(GROUP * CAP, d)
        lse = chunk_stats(factor, x, t, centroids_ref, bias_ref, u_ref, 256)
        lse_ref[2 * t] = lse[:, :128]
        lse_ref[2 * t + 1] = lse[:, 128:]

    wait_bytes(x_ref.at[pl.ds(1, GROUP - 1)], x_in.at[0])
    chunk(0)
    lse_in_ref[0] = lse_ref[0]
    lax.fori_loop(1, GROUP, send_lse, 0)

    def later(t, _):
        wait_bytes(x_ref.at[pl.ds(t * GROUP, GROUP)], x_in.at[t])
        chunk(t)
        lax.fori_loop(t * GROUP, (t + 1) * GROUP, send_lse, 0)
        return 0

    lax.fori_loop(1, PARTS // GROUP, later, 0)
    wait_bytes(lse_in_ref.at[pl.ds(1, PARTS - 1)], lse_in)
    norm = home(mean[:, 0:1], local_sq, lse_in_ref[...].reshape(PARTS, 128), rank_ref, src_ref)
    norm_ref[...] = norm.reshape(norm_ref.shape)
    norm_in_ref[0] = norm_ref[0]

    def send_norm(i, _):
        copy(norm_ref.at[i], norm_in_ref.at[i], norm_out, norm_in, ahead(dp, cent, i)).start()
        return 0

    lax.fori_loop(1, PARTS, send_norm, 0)
    wait_bytes(norm_in_ref.at[pl.ds(1, PARTS - 1)], norm_in)
    log_sum = unpack_norms(dp, cent, norm_in_ref[...].reshape(PARTS, 128), norms_ref)
    energy_ref[...] = jnp.broadcast_to(log_sum * (-1.0 / (energy_scale * rows * PARTS)), energy_ref.shape)
    kb = 256

    def block(b, _):
        ks = pl.ds(pl.multiple_of(b * kb, kb), kb)
        acc = jnp.zeros((kb, d), f32)
        mass = jnp.zeros((kb, 128), f32)
        for t in range(PARTS // GROUP):
            x = x_ref[t * GROUP : (t + 1) * GROUP].reshape(GROUP * CAP, d)
            log = jnp.concatenate([norms_ref[2 * t : 2 * t + 1, :], norms_ref[2 * t + 1 : 2 * t + 2, :]], axis=1)
            w = jnp.exp2(u_ref[t, ks, :] * factor - log).astype(bf16)
            acc = acc + jnp.dot(w, x, preferred_element_type=f32)
            w = w.astype(f32)
            mass = mass + w[:, :128] + w[:, 128:]
        mass = jnp.sum(mass, axis=1, keepdims=True)
        out_ref[ks, :] = (centroids_ref[ks, :].astype(f32) + acc) / (1.0 + mass)
        return 0

    lax.fori_loop(0, n // kb, block, 0)
    wait_bytes(x_ref.at[pl.ds(1, PARTS - 1)], x_out)
    wait_bytes(outer_ref.at[pl.ds(1, OUTER - 1)], sq_out.at[0])
    wait_bytes(inner_ref.at[pl.ds(1, INNER - 1)], sq_out.at[1])
    wait_bytes(lse_in_ref.at[pl.ds(1, PARTS - 1)], lse_out)
    wait_bytes(norm_in_ref.at[pl.ds(1, PARTS - 1)], norm_out)


def body(vectors, owners, centroids, penalty):
    rows, d = vectors.shape
    n = centroids.shape[0]
    shape = jax.ShapeDtypeStruct
    dma = pltpu.SemaphoreType.DMA
    line = (1, 128)
    refined, energy = pl.pallas_call(
        kernel,
        out_shape=(shape((n, d), f32), shape(line, f32)),
        scratch_shapes=[
            pltpu.VMEM((PARTS, CAP, d), bf16),
            pltpu.VMEM((PARTS, CAP, d), bf16),
            pltpu.VMEM((PARTS // GROUP, n, GROUP * CAP), f32),
            pltpu.VMEM((n, 128), f32),
            pltpu.VMEM((PARTS, rows), i32),
            pltpu.VMEM((PARTS, 128), i32),
            pltpu.VMEM((2,) + line, f32),
            pltpu.VMEM((OUTER,) + line, f32),
            pltpu.VMEM((INNER,) + line, f32),
            pltpu.VMEM((PARTS // 4,) + line, f32),
            pltpu.VMEM((PARTS,) + line, f32),
            pltpu.VMEM((PARTS,) + line, f32),
            pltpu.VMEM((PARTS,) + line, f32),
            pltpu.VMEM((PARTS // 4, 128), f32),
            dma,
            dma((PARTS // GROUP,)),
            dma((2,)),
            dma((2,)),
            dma,
            dma,
            dma,
            dma,
        ],
        compiler_params=pltpu.CompilerParams(
            collective_id=0, has_side_effects=True, vmem_limit_bytes=56 * MIB
        ),
    )(owners, vectors, centroids, penalty.reshape(n // 128, 128))
    return refined, energy[0, 0]


def solution(mesh):
    placed = (P(AXES, None), P(AXES, None), P(AXES, None), P(AXES))
    return jax.shard_map(
        body, mesh=mesh, in_specs=placed, out_specs=(P(AXES, None), P()), check_vma=False
    )
```

```python
import math

import jax
import jax.numpy as jnp
from jax import lax
from jax.experimental import pallas as pl
from jax.experimental.pallas import tpu as pltpu
from jax.sharding import PartitionSpec as P

sharpness = 4.0
penalty_weight = 0.5
energy_scale = 16.0

AXES = ("dp", "cent")
CAP = 32
DEAD = 3.0e38
LOG2E = math.log2(math.e)
LN2 = math.log(2.0)
MIB = 1024 * 1024

f32 = jnp.float32
bf16 = jnp.bfloat16
i32 = jnp.int32


def nt(a, b):
    return lax.dot_general(a, b, (((1,), (1,)), ((), ())), preferred_element_type=f32)


def iota(shape, axis):
    return lax.broadcasted_iota(i32, shape, axis)


PARTS = 128
INNER = 16
OUTER = 8
STRIDE = 85
GROUP = 8
GROUPS = PARTS // GROUP
AHEAD = 7
LOGICAL = pl.DeviceIdType.LOGICAL


def jump(i):
    return lax.rem(i * STRIDE, PARTS)


def ahead(dp, cent, i):
    j = jump(i)
    return lax.rem(dp + j // INNER, OUTER) * INNER + lax.rem(cent + lax.rem(j, INNER), INNER)


def behind(dp, cent, i):
    j = jump(i)
    return lax.rem(dp + OUTER - j // INNER, OUTER) * INNER + lax.rem(cent + INNER - lax.rem(j, INNER), INNER)


def arrange(greet, dp, cent, owners_t, vectors_ref, out_ref, rank_ref, src_ref):
    rows = vectors_ref.shape[0]
    step = iota((PARTS, rows), 0)
    j = jnp.bitwise_and(step * STRIDE, PARTS - 1)
    outer = jnp.bitwise_and(dp + jnp.right_shift(j, 4), OUTER - 1)
    part = outer * INNER + jnp.bitwise_and(cent + j, INNER - 1)
    match = part == owners_t[0:1, :]
    for r in range(1, owners_t.shape[0]):
        match = match | (part == owners_t[r : r + 1, :])
    before = jnp.where(iota((rows, rows), 0) < iota((rows, rows), 1), 1.0, 0.0).astype(bf16)
    rank = jnp.dot(jnp.where(match, 1.0, 0.0).astype(bf16), before, preferred_element_type=f32)
    rank_ref[...] = jnp.where(match, rank.astype(i32), -1)
    for g in range(PARTS // GROUP):
        greet(g)
        ranks = rank_ref[g * GROUP : (g + 1) * GROUP, :]
        hot = ranks[:, None, :] == iota((GROUP, CAP, rows), 1)
        hot = jnp.where(hot, 1.0, 0.0).astype(bf16).reshape(GROUP * CAP, rows)
        picked = jnp.dot(hot, vectors_ref[...], preferred_element_type=f32).astype(bf16)
        out_ref[g * GROUP : (g + 1) * GROUP] = picked.reshape(GROUP, CAP, picked.shape[1])


def invert_ranks(rank_ref, src_ref):
    rows = rank_ref.shape[1]
    ranks = rank_ref[...]
    row = iota((PARTS, rows), 1)
    slot = iota((PARTS, 128), 1) - jnp.bitwise_and(iota((PARTS, 128), 0), 3) * CAP
    src = jnp.full((PARTS, 128), -1, i32)
    for j in range(CAP):
        here = jnp.max(jnp.where(ranks == j, row, -1), axis=1, keepdims=True)
        src = jnp.where(slot == j, here, src)
    src_ref[...] = src


def fill_bias(mean, centroids_ref, penalty_ref, bias_ref):
    n = centroids_ref.shape[0]
    eye = iota((128, 128), 0) == iota((128, 128), 1)
    for g in range(n // 128):
        c = centroids_ref[g * 128 : (g + 1) * 128, :].astype(f32)
        c = c * c
        half = sum(c[:, i : i + 128] for i in range(0, c.shape[1], 128)) * 0.5
        pen = penalty_ref[g : g + 1, :].astype(f32) * (penalty_weight * sharpness * 0.5) * mean
        col = jnp.sum(half + jnp.where(eye, pen, 0.0), axis=1, keepdims=True)
        bias_ref[g * 128 : (g + 1) * 128, :] = jnp.broadcast_to(col, (128, 128))


def chunk_stats(factor, x, t, centroids_ref, bias_ref, u_ref, kb):
    n = centroids_ref.shape[0]
    width = x.shape[0]
    peak = jnp.full((8, width), -DEAD, f32)
    for k in range(0, n, kb):
        b = bias_ref[k : k + kb, :]
        u = nt(centroids_ref[k : k + kb, :], x) - jnp.concatenate([b, b], axis=1)
        u_ref[t, k : k + kb, :] = u
        peak = jnp.maximum(peak, jnp.max(u.reshape(kb // 8, 8, width), axis=0))
    peak = jnp.max(peak, axis=0, keepdims=True)
    total = jnp.zeros((8, width), f32)
    for k in range(0, n, kb):
        p = jnp.exp2((u_ref[t, k : k + kb, :] - peak) * factor)
        total = total + jnp.sum(p.reshape(kb // 8, 8, width), axis=0)
    return peak * factor + jnp.log2(jnp.sum(total, axis=0, keepdims=True))


def home(mean, local_sq, lse, rank_ref, src_ref):
    rows = rank_ref.shape[1]
    quarter = jnp.bitwise_and(iota((PARTS, 128), 0), 3) * CAP
    logs = []
    for h in range(0, rows, 128):
        ranks = rank_ref[:, h : h + 128]
        live = ranks >= 0
        got = jnp.take_along_axis(lse, jnp.maximum(ranks, 0) + quarter, axis=1)
        peak = jnp.max(jnp.where(live, got, -DEAD), axis=0, keepdims=True)
        total = jnp.sum(jnp.where(live, jnp.exp2(got - peak), 0.0), axis=0, keepdims=True)
        logs.append(peak + jnp.log2(total))
    src = src_ref[...]
    norm = jnp.full((PARTS, 128), DEAD, f32)
    for h, log in enumerate(logs):
        got = jnp.take_along_axis(jnp.broadcast_to(log, (PARTS, 128)), jnp.bitwise_and(src, 127), axis=1)
        norm = jnp.where((src >= h * 128) & (src < (h + 1) * 128), got, norm)
    log_sum = LN2 * jnp.sum(sum(logs), axis=1, keepdims=True) - local_sq / (sharpness * mean)
    spare = jnp.bitwise_and(quarter + CAP, 127)
    return jnp.where(iota((PARTS, 128), 1) == spare, log_sum, norm)


def sum_logs(dp, cent, norm):
    lane = iota((PARTS, 128), 1)
    j = jnp.bitwise_and(iota((PARTS, 128), 0) * STRIDE, PARTS - 1)
    outer = jnp.bitwise_and(dp + OUTER - jnp.right_shift(j, 4), OUTER - 1)
    sender = outer * INNER + jnp.bitwise_and(cent + PARTS - j, INNER - 1)
    quarter = jnp.bitwise_and(iota((PARTS, 128), 0), 3) * CAP
    spare = jnp.bitwise_and(quarter + CAP, 127)
    log_sum = jnp.sum(jnp.where(lane == spare, norm, 0.0), axis=1, keepdims=True)
    log_sum = jnp.sum(jnp.where(lane == sender, log_sum, 0.0), axis=0, keepdims=True)
    log_sum = jnp.sum(log_sum, axis=1, keepdims=True)
    return log_sum


def unpack_norms(norm_in_ref, norms_ref, half):
    count = PARTS // 2
    norm = norm_in_ref[half * count : (half + 1) * count].reshape(count, 128)
    quarter = jnp.bitwise_and(iota((count, 128), 0), 3) * CAP
    mine = jnp.where(jnp.bitwise_and(iota((count, 128), 1), 96) == quarter, norm, 0.0)
    norms_ref[half * count // 4 : (half + 1) * count // 4, :] = jnp.sum(mine.reshape(count // 4, 4, 128), axis=1)


def kernel(
    owners_ref, vectors_ref, centroids_ref, penalty_ref, out_ref, energy_ref,
    send_ref, x_ref, u_ref, bias_ref, rank_ref, src_ref,
    sq_ref, outer_ref, inner_ref, lse_ref, lse_in_ref, norm_ref, norm_in_ref, norms_ref, mass_ref,
    x_out, x_in, sq_out, sq_in, lse_out, lse_in, norm_out, norm_in,
):
    dp, cent = lax.axis_index("dp"), lax.axis_index("cent")
    n, d = centroids_ref.shape
    rows = vectors_ref.shape[0]
    barrier = pltpu.get_barrier_semaphore()

    def greet(g):
        for i in range(g * GROUP, (g + 1) * GROUP):
            if i > 0:
                pl.semaphore_signal(barrier, inc=1, device_id=ahead(dp, cent, i), device_id_type=LOGICAL)

    arrange(greet, dp, cent, owners_ref[...], vectors_ref, send_ref, rank_ref, src_ref)
    x_ref[0] = send_ref[0]
    v = vectors_ref[...].astype(f32)
    local_sq = jnp.sum(jnp.sum(v * v, axis=0, keepdims=True), axis=1, keepdims=True)
    sq_ref[0] = jnp.broadcast_to(local_sq, (1, 128))
    outer_ref[0] = sq_ref[0]
    pl.semaphore_wait(barrier, PARTS - 1)

    def copy(src, dst, out_sem, in_sem, device):
        return pltpu.make_async_remote_copy(
            src_ref=src, dst_ref=dst, send_sem=out_sem, recv_sem=in_sem, device_id=device, device_id_type=LOGICAL
        )

    def wait_bytes(ref, sem):
        pltpu.make_async_copy(ref, ref, sem).wait()

    for i in range(1, OUTER):
        device = lax.rem(dp + i, OUTER) * INNER + cent
        copy(sq_ref.at[0], outer_ref.at[i], sq_out.at[0], sq_in.at[0], device).start()

    def send_group(g):
        for k in range(GROUP):
            i = g * GROUP + k
            if isinstance(g, int) and i == 0:
                continue
            copy(send_ref.at[i], x_ref.at[i], x_out.at[g], x_in.at[g], ahead(dp, cent, i)).start()

    for g in range(AHEAD):
        send_group(g)
    wait_bytes(outer_ref.at[pl.ds(1, OUTER - 1)], sq_in.at[0])
    sq_ref[1] = jnp.sum(outer_ref[...], axis=0)
    inner_ref[0] = sq_ref[1]
    for i in range(1, INNER):
        device = dp * INNER + lax.rem(cent + i, INNER)
        copy(sq_ref.at[1], inner_ref.at[i], sq_out.at[1], sq_in.at[1], device).start()
    invert_ranks(rank_ref, src_ref)
    wait_bytes(inner_ref.at[pl.ds(1, INNER - 1)], sq_in.at[1])
    mean = jnp.sum(inner_ref[...], axis=0) * (1.0 / (rows * PARTS * d))
    fill_bias(mean, centroids_ref, penalty_ref, bias_ref)
    factor = LOG2E * 2.0 / (sharpness * mean)
    factor = jnp.concatenate([factor, factor], axis=1)

    def send_lse(t):
        for k in range(GROUP):
            i = t * GROUP + k
            if isinstance(t, int) and i == 0:
                continue
            copy(lse_ref.at[t * 2 + k // 4], lse_in_ref.at[i], lse_out, lse_in, behind(dp, cent, i)).start()

    def chunk(t):
        x = x_ref[pl.ds(t * GROUP, GROUP)].reshape(GROUP * CAP, d)
        lse = chunk_stats(factor, x, t, centroids_ref, bias_ref, u_ref, 256)
        lse_ref[2 * t] = lse[:, :128]
        lse_ref[2 * t + 1] = lse[:, 128:]

    wait_bytes(x_ref.at[pl.ds(1, GROUP - 1)], x_out.at[0])
    send_group(AHEAD)
    wait_bytes(x_ref.at[pl.ds(1, GROUP - 1)], x_in.at[0])
    chunk(0)
    lse_in_ref[0] = lse_ref[0]
    send_lse(0)

    def later(t, _):
        group = x_ref.at[pl.ds(t * GROUP, GROUP)]
        wait_bytes(group, x_out.at[t])

        @pl.when(t < GROUPS - AHEAD)
        def _():
            send_group(t + AHEAD)

        wait_bytes(group, x_in.at[t])
        chunk(t)
        send_lse(t)
        return 0

    lax.fori_loop(1, GROUPS, later, 0)
    wait_bytes(lse_in_ref.at[pl.ds(1, PARTS - 1)], lse_in)
    norm = home(mean[:, 0:1], local_sq, lse_in_ref[...].reshape(PARTS, 128), rank_ref, src_ref)
    norm_ref[...] = norm.reshape(norm_ref.shape)
    norm_in_ref[0] = norm_ref[0]

    def send_norm(half):
        def one(i, _):
            copy(norm_ref.at[i], norm_in_ref.at[i], norm_out, norm_in.at[half], ahead(dp, cent, i)).start()
            return 0

        return one

    lax.fori_loop(1, PARTS // 2, send_norm(0), 0, unroll=4)
    lax.fori_loop(PARTS // 2, PARTS, send_norm(1), 0, unroll=4)
    kb = 256

    def block(half):
        def run(b, _):
            ks = pl.ds(pl.multiple_of(b * kb, kb), kb)
            acc = jnp.zeros((kb, d), f32)
            mass = jnp.zeros((kb, 128), f32)
            for t in range(half * GROUPS // 2, (half + 1) * GROUPS // 2):
                x = x_ref[t * GROUP : (t + 1) * GROUP].reshape(GROUP * CAP, d)
                log = jnp.concatenate([norms_ref[2 * t : 2 * t + 1, :], norms_ref[2 * t + 1 : 2 * t + 2, :]], axis=1)
                w = jnp.exp2(u_ref[t, ks, :] * factor - log).astype(bf16)
                acc = acc + jnp.dot(w, x, preferred_element_type=f32)
                w = w.astype(f32)
                mass = mass + w[:, :128] + w[:, 128:]
            if half == 0:
                out_ref[ks, :] = acc
                mass_ref[ks, :] = mass
            else:
                mass = jnp.sum(mass + mass_ref[ks, :], axis=1, keepdims=True)
                out_ref[ks, :] = (centroids_ref[ks, :].astype(f32) + (acc + out_ref[ks, :])) / (1.0 + mass)
            return 0

        return run

    wait_bytes(norm_in_ref.at[pl.ds(1, PARTS // 2 - 1)], norm_in.at[0])
    unpack_norms(norm_in_ref, norms_ref, 0)
    lax.fori_loop(0, n // kb, block(0), 0)
    wait_bytes(norm_in_ref.at[pl.ds(PARTS // 2, PARTS // 2)], norm_in.at[1])
    unpack_norms(norm_in_ref, norms_ref, 1)
    log_sum = sum_logs(dp, cent, norm_in_ref[...].reshape(PARTS, 128))
    energy_ref[...] = jnp.broadcast_to(log_sum * (-1.0 / (energy_scale * rows * PARTS)), energy_ref.shape)
    lax.fori_loop(0, n // kb, block(1), 0)
    wait_bytes(outer_ref.at[pl.ds(1, OUTER - 1)], sq_out.at[0])
    wait_bytes(inner_ref.at[pl.ds(1, INNER - 1)], sq_out.at[1])
    wait_bytes(lse_in_ref.at[pl.ds(1, PARTS - 1)], lse_out)
    wait_bytes(norm_in_ref.at[pl.ds(1, PARTS - 1)], norm_out)


def body(vectors, owners, centroids, penalty):
    rows, d = vectors.shape
    n = centroids.shape[0]
    shape = jax.ShapeDtypeStruct
    dma = pltpu.SemaphoreType.DMA
    line = (1, 128)
    refined, energy = pl.pallas_call(
        kernel,
        out_shape=(shape((n, d), f32), shape(line, f32)),
        scratch_shapes=[
            pltpu.VMEM((PARTS, CAP, d), bf16),
            pltpu.VMEM((PARTS, CAP, d), bf16),
            pltpu.VMEM((PARTS // GROUP, n, GROUP * CAP), f32),
            pltpu.VMEM((n, 128), f32),
            pltpu.VMEM((PARTS, rows), i32),
            pltpu.VMEM((PARTS, 128), i32),
            pltpu.VMEM((2,) + line, f32),
            pltpu.VMEM((OUTER,) + line, f32),
            pltpu.VMEM((INNER,) + line, f32),
            pltpu.VMEM((PARTS // 4,) + line, f32),
            pltpu.VMEM((PARTS,) + line, f32),
            pltpu.VMEM((PARTS,) + line, f32),
            pltpu.VMEM((PARTS,) + line, f32),
            pltpu.VMEM((PARTS // 4, 128), f32),
            pltpu.VMEM((n, 128), f32),
            dma((GROUPS,)),
            dma((GROUPS,)),
            dma((2,)),
            dma((2,)),
            dma,
            dma,
            dma,
            dma((2,)),
        ],
        compiler_params=pltpu.CompilerParams(
            collective_id=0, has_side_effects=True, vmem_limit_bytes=56 * MIB
        ),
    )(owners.T, vectors, centroids, penalty.reshape(n // 128, 128))
    return refined, energy[0, 0]


def solution(mesh):
    placed = (P(AXES, None), P(AXES, None), P(AXES, None), P(AXES))
    return jax.shard_map(
        body, mesh=mesh, in_specs=placed, out_specs=(P(AXES, None), P()), check_vma=False
    )
```

```python
import math

import jax
import jax.numpy as jnp
from jax import lax
from jax.experimental import pallas as pl
from jax.experimental.pallas import tpu as pltpu
from jax.sharding import PartitionSpec as P

sharpness = 4.0
penalty_weight = 0.5
energy_scale = 16.0

AXES = ("dp", "cent")
CAP = 32
DEAD = 3.0e38
LOG2E = math.log2(math.e)
LN2 = math.log(2.0)
MIB = 1024 * 1024

f32 = jnp.float32
bf16 = jnp.bfloat16
i32 = jnp.int32


def nt(a, b):
    return lax.dot_general(a, b, (((1,), (1,)), ((), ())), preferred_element_type=f32)


def iota(shape, axis):
    return lax.broadcasted_iota(i32, shape, axis)


PARTS = 128
INNER = 16
OUTER = 8
STRIDE = 85
GROUP = 8
GROUPS = PARTS // GROUP
AHEAD = 7
LOGICAL = pl.DeviceIdType.LOGICAL


def jump(i):
    return lax.rem(i * STRIDE, PARTS)


def ahead(dp, cent, i):
    j = jump(i)
    return lax.rem(dp + j // INNER, OUTER) * INNER + lax.rem(cent + lax.rem(j, INNER), INNER)


def behind(dp, cent, i):
    j = jump(i)
    return lax.rem(dp + OUTER - j // INNER, OUTER) * INNER + lax.rem(cent + INNER - lax.rem(j, INNER), INNER)


def arrange(greet, dp, cent, owners_t, vectors_ref, out_ref, rank_ref, src_ref):
    rows = vectors_ref.shape[0]
    step = iota((PARTS, rows), 0)
    j = jnp.bitwise_and(step * STRIDE, PARTS - 1)
    outer = jnp.bitwise_and(dp + jnp.right_shift(j, 4), OUTER - 1)
    part = outer * INNER + jnp.bitwise_and(cent + j, INNER - 1)
    match = part == owners_t[0:1, :]
    for r in range(1, owners_t.shape[0]):
        match = match | (part == owners_t[r : r + 1, :])
    before = jnp.where(iota((rows, rows), 0) < iota((rows, rows), 1), 1.0, 0.0).astype(bf16)
    rank = jnp.dot(jnp.where(match, 1.0, 0.0).astype(bf16), before, preferred_element_type=f32)
    rank_ref[...] = jnp.where(match, rank.astype(i32), -1)
    for g in range(PARTS // GROUP):
        greet(g)
        ranks = rank_ref[g * GROUP : (g + 1) * GROUP, :]
        hot = ranks[:, None, :] == iota((GROUP, CAP, rows), 1)
        hot = jnp.where(hot, 1.0, 0.0).astype(bf16).reshape(GROUP * CAP, rows)
        picked = jnp.dot(hot, vectors_ref[...], preferred_element_type=f32).astype(bf16)
        out_ref[g * GROUP : (g + 1) * GROUP] = picked.reshape(GROUP, CAP, picked.shape[1])


def invert_ranks(rank_ref, src_ref):
    rows = rank_ref.shape[1]
    ranks = rank_ref[...]
    row = iota((PARTS, rows), 1)
    slot = iota((PARTS, 128), 1) - jnp.bitwise_and(iota((PARTS, 128), 0), 3) * CAP
    src = jnp.full((PARTS, 128), -1, i32)
    for j in range(CAP):
        here = jnp.max(jnp.where(ranks == j, row, -1), axis=1, keepdims=True)
        src = jnp.where(slot == j, here, src)
    src_ref[...] = src


def fill_bias(mean, centroids_ref, penalty_ref, bias_ref):
    n = centroids_ref.shape[0]
    eye = iota((128, 128), 0) == iota((128, 128), 1)
    for g in range(n // 128):
        c = centroids_ref[g * 128 : (g + 1) * 128, :].astype(f32)
        c = c * c
        half = sum(c[:, i : i + 128] for i in range(0, c.shape[1], 128)) * 0.5
        pen = penalty_ref[g : g + 1, :].astype(f32) * (penalty_weight * sharpness * 0.5) * mean
        col = jnp.sum(half + jnp.where(eye, pen, 0.0), axis=1, keepdims=True)
        bias_ref[g * 128 : (g + 1) * 128, :] = jnp.broadcast_to(col, (128, 128))


def chunk_stats(factor, x, t, centroids_ref, bias_ref, u_ref, kb):
    n = centroids_ref.shape[0]
    width = x.shape[0]
    peak = jnp.full((8, width), -DEAD, f32)
    for k in range(0, n, kb):
        b = bias_ref[k : k + kb, :]
        u = nt(centroids_ref[k : k + kb, :], x) - jnp.concatenate([b, b], axis=1)
        u_ref[t, k : k + kb, :] = u
        peak = jnp.maximum(peak, jnp.max(u.reshape(kb // 8, 8, width), axis=0))
    peak = jnp.max(peak, axis=0, keepdims=True)
    total = jnp.zeros((8, width), f32)
    for k in range(0, n, kb):
        p = jnp.exp2((u_ref[t, k : k + kb, :] - peak) * factor)
        u_ref[t, k : k + kb, :] = p
        total = total + jnp.sum(p.reshape(kb // 8, 8, width), axis=0)
    peak = peak * factor
    return peak, peak + jnp.log2(jnp.sum(total, axis=0, keepdims=True))


def home(mean, local_sq, lse, rank_ref, src_ref):
    rows = rank_ref.shape[1]
    quarter = jnp.bitwise_and(iota((PARTS, 128), 0), 3) * CAP
    logs = []
    for h in range(0, rows, 128):
        ranks = rank_ref[:, h : h + 128]
        live = ranks >= 0
        got = jnp.take_along_axis(lse, jnp.maximum(ranks, 0) + quarter, axis=1)
        peak = jnp.max(jnp.where(live, got, -DEAD), axis=0, keepdims=True)
        total = jnp.sum(jnp.where(live, jnp.exp2(got - peak), 0.0), axis=0, keepdims=True)
        logs.append(peak + jnp.log2(total))
    src = src_ref[...]
    norm = jnp.full((PARTS, 128), DEAD, f32)
    for h, log in enumerate(logs):
        got = jnp.take_along_axis(jnp.broadcast_to(log, (PARTS, 128)), jnp.bitwise_and(src, 127), axis=1)
        norm = jnp.where((src >= h * 128) & (src < (h + 1) * 128), got, norm)
    log_sum = LN2 * jnp.sum(sum(logs), axis=1, keepdims=True) - local_sq / (sharpness * mean)
    spare = jnp.bitwise_and(quarter + CAP, 127)
    return jnp.where(iota((PARTS, 128), 1) == spare, log_sum, norm)


def sum_logs(dp, cent, norm):
    lane = iota((PARTS, 128), 1)
    j = jnp.bitwise_and(iota((PARTS, 128), 0) * STRIDE, PARTS - 1)
    outer = jnp.bitwise_and(dp + OUTER - jnp.right_shift(j, 4), OUTER - 1)
    sender = outer * INNER + jnp.bitwise_and(cent + PARTS - j, INNER - 1)
    quarter = jnp.bitwise_and(iota((PARTS, 128), 0), 3) * CAP
    spare = jnp.bitwise_and(quarter + CAP, 127)
    log_sum = jnp.sum(jnp.where(lane == spare, norm, 0.0), axis=1, keepdims=True)
    log_sum = jnp.sum(jnp.where(lane == sender, log_sum, 0.0), axis=0, keepdims=True)
    log_sum = jnp.sum(log_sum, axis=1, keepdims=True)
    return log_sum


def unpack_norms(norm_in_ref, norms_ref, peak_ref, half):
    count = PARTS // 2
    norm = norm_in_ref[half * count : (half + 1) * count].reshape(count, 128)
    quarter = jnp.bitwise_and(iota((count, 128), 0), 3) * CAP
    mine = jnp.where(jnp.bitwise_and(iota((count, 128), 1), 96) == quarter, norm, 0.0)
    norms_ref[half * count // 4 : (half + 1) * count // 4, :] = jnp.sum(mine.reshape(count // 4, 4, 128), axis=1)
    for t in range(half * GROUPS // 2, (half + 1) * GROUPS // 2):
        norm = jnp.concatenate([norms_ref[2 * t : 2 * t + 1, :], norms_ref[2 * t + 1 : 2 * t + 2, :]], axis=1)
        peak_ref[t] = jnp.exp2(peak_ref[t] - norm)


def kernel(
    owners_ref, vectors_ref, centroids_ref, penalty_ref, out_ref, energy_ref,
    send_ref, x_ref, u_ref, bias_ref, rank_ref, src_ref,
    sq_ref, outer_ref, inner_ref, lse_ref, lse_in_ref, norm_ref, norm_in_ref, norms_ref, mass_ref, peak_ref,
    x_out, x_in, sq_out, sq_in, lse_out, lse_in, norm_out, norm_in,
):
    dp, cent = lax.axis_index("dp"), lax.axis_index("cent")
    n, d = centroids_ref.shape
    rows = vectors_ref.shape[0]
    barrier = pltpu.get_barrier_semaphore()

    def greet(g):
        for i in range(g * GROUP, (g + 1) * GROUP):
            if i > 0:
                pl.semaphore_signal(barrier, inc=1, device_id=ahead(dp, cent, i), device_id_type=LOGICAL)

    arrange(greet, dp, cent, owners_ref[...], vectors_ref, send_ref, rank_ref, src_ref)
    x_ref[0] = send_ref[0]
    v = vectors_ref[...].astype(f32)
    local_sq = jnp.sum(jnp.sum(v * v, axis=0, keepdims=True), axis=1, keepdims=True)
    sq_ref[0] = jnp.broadcast_to(local_sq, (1, 128))
    outer_ref[0] = sq_ref[0]
    pl.semaphore_wait(barrier, PARTS - 1)

    def copy(src, dst, out_sem, in_sem, device):
        return pltpu.make_async_remote_copy(
            src_ref=src, dst_ref=dst, send_sem=out_sem, recv_sem=in_sem, device_id=device, device_id_type=LOGICAL
        )

    def wait_bytes(ref, sem):
        pltpu.make_async_copy(ref, ref, sem).wait()

    for i in range(1, OUTER):
        device = lax.rem(dp + i, OUTER) * INNER + cent
        copy(sq_ref.at[0], outer_ref.at[i], sq_out.at[0], sq_in.at[0], device).start()

    def send_group(g):
        for k in range(GROUP):
            i = g * GROUP + k
            if isinstance(g, int) and i == 0:
                continue
            copy(send_ref.at[i], x_ref.at[i], x_out.at[g], x_in.at[g], ahead(dp, cent, i)).start()

    for g in range(AHEAD):
        send_group(g)
    wait_bytes(outer_ref.at[pl.ds(1, OUTER - 1)], sq_in.at[0])
    sq_ref[1] = jnp.sum(outer_ref[...], axis=0)
    inner_ref[0] = sq_ref[1]
    for i in range(1, INNER):
        device = dp * INNER + lax.rem(cent + i, INNER)
        copy(sq_ref.at[1], inner_ref.at[i], sq_out.at[1], sq_in.at[1], device).start()
    invert_ranks(rank_ref, src_ref)
    wait_bytes(inner_ref.at[pl.ds(1, INNER - 1)], sq_in.at[1])
    mean = jnp.sum(inner_ref[...], axis=0) * (1.0 / (rows * PARTS * d))
    fill_bias(mean, centroids_ref, penalty_ref, bias_ref)
    factor = LOG2E * 2.0 / (sharpness * mean)
    factor = jnp.concatenate([factor, factor], axis=1)

    def send_lse(t):
        for k in range(GROUP):
            i = t * GROUP + k
            if isinstance(t, int) and i == 0:
                continue
            copy(lse_ref.at[t * 2 + k // 4], lse_in_ref.at[i], lse_out, lse_in, behind(dp, cent, i)).start()

    def chunk(t):
        x = x_ref[pl.ds(t * GROUP, GROUP)].reshape(GROUP * CAP, d)
        peak, lse = chunk_stats(factor, x, t, centroids_ref, bias_ref, u_ref, 256)
        peak_ref[t] = peak
        lse_ref[2 * t] = lse[:, :128]
        lse_ref[2 * t + 1] = lse[:, 128:]

    wait_bytes(x_ref.at[pl.ds(1, GROUP - 1)], x_out.at[0])
    send_group(AHEAD)
    wait_bytes(x_ref.at[pl.ds(1, GROUP - 1)], x_in.at[0])
    chunk(0)
    lse_in_ref[0] = lse_ref[0]
    send_lse(0)

    def later(t, _):
        group = x_ref.at[pl.ds(t * GROUP, GROUP)]
        wait_bytes(group, x_out.at[t])

        @pl.when(t < GROUPS - AHEAD)
        def _():
            send_group(t + AHEAD)

        wait_bytes(group, x_in.at[t])
        chunk(t)
        send_lse(t)
        return 0

    lax.fori_loop(1, GROUPS, later, 0)
    wait_bytes(lse_in_ref.at[pl.ds(1, PARTS - 1)], lse_in)
    norm = home(mean[:, 0:1], local_sq, lse_in_ref[...].reshape(PARTS, 128), rank_ref, src_ref)
    norm_ref[...] = norm.reshape(norm_ref.shape)
    norm_in_ref[0] = norm_ref[0]

    def send_norm(half):
        def one(i, _):
            copy(norm_ref.at[i], norm_in_ref.at[i], norm_out, norm_in.at[half], ahead(dp, cent, i)).start()
            return 0

        return one

    lax.fori_loop(1, PARTS // 2, send_norm(0), 0, unroll=4)
    lax.fori_loop(PARTS // 2, PARTS, send_norm(1), 0, unroll=4)
    kb = 256

    def block(half):
        def run(b, _):
            ks = pl.ds(pl.multiple_of(b * kb, kb), kb)
            acc = jnp.zeros((kb, d), f32)
            mass = jnp.zeros((kb, 128), f32)
            for t in range(half * GROUPS // 2, (half + 1) * GROUPS // 2):
                x = x_ref[t * GROUP : (t + 1) * GROUP].reshape(GROUP * CAP, d)
                w = (u_ref[t, ks, :] * peak_ref[t]).astype(bf16)
                acc = acc + jnp.dot(w, x, preferred_element_type=f32)
                w = w.astype(f32)
                mass = mass + w[:, :128] + w[:, 128:]
            if half == 0:
                out_ref[ks, :] = acc
                mass_ref[ks, :] = mass
            else:
                mass = jnp.sum(mass + mass_ref[ks, :], axis=1, keepdims=True)
                out_ref[ks, :] = (centroids_ref[ks, :].astype(f32) + (acc + out_ref[ks, :])) / (1.0 + mass)
            return 0

        return run

    wait_bytes(norm_in_ref.at[pl.ds(1, PARTS // 2 - 1)], norm_in.at[0])
    unpack_norms(norm_in_ref, norms_ref, peak_ref, 0)
    lax.fori_loop(0, n // kb, block(0), 0)
    wait_bytes(norm_in_ref.at[pl.ds(PARTS // 2, PARTS // 2)], norm_in.at[1])
    unpack_norms(norm_in_ref, norms_ref, peak_ref, 1)
    log_sum = sum_logs(dp, cent, norm_in_ref[...].reshape(PARTS, 128))
    energy_ref[...] = jnp.broadcast_to(log_sum * (-1.0 / (energy_scale * rows * PARTS)), energy_ref.shape)
    lax.fori_loop(0, n // kb, block(1), 0)
    wait_bytes(outer_ref.at[pl.ds(1, OUTER - 1)], sq_out.at[0])
    wait_bytes(inner_ref.at[pl.ds(1, INNER - 1)], sq_out.at[1])
    wait_bytes(lse_in_ref.at[pl.ds(1, PARTS - 1)], lse_out)
    wait_bytes(norm_in_ref.at[pl.ds(1, PARTS - 1)], norm_out)


def body(vectors, owners, centroids, penalty):
    rows, d = vectors.shape
    n = centroids.shape[0]
    shape = jax.ShapeDtypeStruct
    dma = pltpu.SemaphoreType.DMA
    line = (1, 128)
    refined, energy = pl.pallas_call(
        kernel,
        out_shape=(pltpu.VMEM((n, d), f32), shape(line, f32)),
        scratch_shapes=[
            pltpu.VMEM((PARTS, CAP, d), bf16),
            pltpu.VMEM((PARTS, CAP, d), bf16),
            pltpu.VMEM((PARTS // GROUP, n, GROUP * CAP), f32),
            pltpu.VMEM((n, 128), f32),
            pltpu.VMEM((PARTS, rows), i32),
            pltpu.VMEM((PARTS, 128), i32),
            pltpu.VMEM((2,) + line, f32),
            pltpu.VMEM((OUTER,) + line, f32),
            pltpu.VMEM((INNER,) + line, f32),
            pltpu.VMEM((PARTS // 4,) + line, f32),
            pltpu.VMEM((PARTS,) + line, f32),
            pltpu.VMEM((PARTS,) + line, f32),
            pltpu.VMEM((PARTS,) + line, f32),
            pltpu.VMEM((PARTS // 4, 128), f32),
            pltpu.VMEM((n, 128), f32),
            pltpu.VMEM((GROUPS, 1, GROUP * CAP), f32),
            dma((GROUPS,)),
            dma((GROUPS,)),
            dma((2,)),
            dma((2,)),
            dma,
            dma,
            dma,
            dma((2,)),
        ],
        compiler_params=pltpu.CompilerParams(
            collective_id=0, has_side_effects=True, vmem_limit_bytes=48 * MIB
        ),
    )(owners.T, vectors, centroids, penalty.reshape(n // 128, 128))
    return refined, energy[0, 0]


def solution(mesh):
    placed = (P(AXES, None), P(AXES, None), P(AXES, None), P(AXES))
    return jax.shard_map(
        body, mesh=mesh, in_specs=placed, out_specs=(P(AXES, None), P()), check_vma=False
    )
```

```python
import math

import jax
import jax.numpy as jnp
from jax import lax
from jax.experimental import pallas as pl
from jax.experimental.pallas import tpu as pltpu
from jax.sharding import PartitionSpec as P

sharpness = 4.0
penalty_weight = 0.5
energy_scale = 16.0

AXES = ("dp", "cent")
CAP = 32
DEAD = 3.0e38
LOG2E = math.log2(math.e)
LN2 = math.log(2.0)
MIB = 1024 * 1024

f32 = jnp.float32
bf16 = jnp.bfloat16
i32 = jnp.int32


def nt(a, b):
    return lax.dot_general(a, b, (((1,), (1,)), ((), ())), preferred_element_type=f32)


def iota(shape, axis):
    return lax.broadcasted_iota(i32, shape, axis)


PARTS = 128
INNER = 16
OUTER = 8
STRIDE = 85
GROUP = 8
GROUPS = PARTS // GROUP
AHEAD = 7
LOGICAL = pl.DeviceIdType.LOGICAL


def jump(i):
    return lax.rem(i * STRIDE, PARTS)


def ahead(dp, cent, i):
    j = jump(i)
    return lax.rem(dp + j // INNER, OUTER) * INNER + lax.rem(cent + lax.rem(j, INNER), INNER)


def behind(dp, cent, i):
    j = jump(i)
    return lax.rem(dp + OUTER - j // INNER, OUTER) * INNER + lax.rem(cent + INNER - lax.rem(j, INNER), INNER)


def arrange(greet, dp, cent, owners_t, vectors_ref, out_ref, rank_ref, src_ref):
    rows = vectors_ref.shape[0]
    step = iota((PARTS, rows), 0)
    j = jnp.bitwise_and(step * STRIDE, PARTS - 1)
    outer = jnp.bitwise_and(dp + jnp.right_shift(j, 4), OUTER - 1)
    part = outer * INNER + jnp.bitwise_and(cent + j, INNER - 1)
    match = part == owners_t[0:1, :]
    for r in range(1, owners_t.shape[0]):
        match = match | (part == owners_t[r : r + 1, :])
    before = jnp.where(iota((rows, rows), 0) < iota((rows, rows), 1), 1.0, 0.0).astype(bf16)
    rank = jnp.dot(jnp.where(match, 1.0, 0.0).astype(bf16), before, preferred_element_type=f32)
    rank_ref[...] = jnp.where(match, rank.astype(i32), -1)
    for g in range(PARTS // GROUP):
        greet(g)
        ranks = rank_ref[g * GROUP : (g + 1) * GROUP, :]
        hot = ranks[:, None, :] == iota((GROUP, CAP, rows), 1)
        hot = jnp.where(hot, 1.0, 0.0).astype(bf16).reshape(GROUP * CAP, rows)
        picked = jnp.dot(hot, vectors_ref[...], preferred_element_type=f32).astype(bf16)
        out_ref[g * GROUP : (g + 1) * GROUP] = picked.reshape(GROUP, CAP, picked.shape[1])


def invert_ranks(rank_ref, src_ref):
    rows = rank_ref.shape[1]
    ranks = rank_ref[...]
    row = iota((PARTS, rows), 1)
    slot = iota((PARTS, 128), 1) - jnp.bitwise_and(iota((PARTS, 128), 0), 3) * CAP
    src = jnp.full((PARTS, 128), -1, i32)
    for j in range(CAP):
        here = jnp.max(jnp.where(ranks == j, row, -1), axis=1, keepdims=True)
        src = jnp.where(slot == j, here, src)
    src_ref[...] = src


def fill_bias(mean, centroids_ref, penalty_ref, bias_ref):
    n = centroids_ref.shape[0]
    eye = iota((128, 128), 0) == iota((128, 128), 1)
    for g in range(n // 128):
        c = centroids_ref[g * 128 : (g + 1) * 128, :].astype(f32)
        c = c * c
        half = sum(c[:, i : i + 128] for i in range(0, c.shape[1], 128)) * 0.5
        pen = penalty_ref[g : g + 1, :].astype(f32) * (penalty_weight * sharpness * 0.5) * mean
        col = jnp.sum(half + jnp.where(eye, pen, 0.0), axis=1, keepdims=True)
        bias_ref[g * 128 : (g + 1) * 128, :] = jnp.broadcast_to(col, (128, 128))


def chunk_stats(factor, x, t, centroids_ref, bias_ref, u_ref, kb):
    n = centroids_ref.shape[0]
    width = x.shape[0]
    peak = jnp.full((8, width), -DEAD, f32)
    for k in range(0, n, kb):
        b = bias_ref[k : k + kb, :]
        u = nt(centroids_ref[k : k + kb, :], x) - jnp.concatenate([b, b], axis=1)
        u_ref[t, k : k + kb, :] = u
        peak = jnp.maximum(peak, jnp.max(u.reshape(kb // 8, 8, width), axis=0))
    peak = jnp.max(peak, axis=0, keepdims=True)
    total = jnp.zeros((8, width), f32)
    for k in range(0, n, kb):
        p = jnp.exp2((u_ref[t, k : k + kb, :] - peak) * factor)
        u_ref[t, k : k + kb, :] = p
        total = total + jnp.sum(p.reshape(kb // 8, 8, width), axis=0)
    peak = peak * factor
    return peak, peak + jnp.log2(jnp.sum(total, axis=0, keepdims=True))


def home(mean, local_sq, lse, rank_ref, src_ref):
    rows = rank_ref.shape[1]
    quarter = jnp.bitwise_and(iota((PARTS, 128), 0), 3) * CAP
    logs = []
    for h in range(0, rows, 128):
        ranks = rank_ref[:, h : h + 128]
        live = ranks >= 0
        got = jnp.take_along_axis(lse, jnp.maximum(ranks, 0) + quarter, axis=1)
        peak = jnp.max(jnp.where(live, got, -DEAD), axis=0, keepdims=True)
        total = jnp.sum(jnp.where(live, jnp.exp2(got - peak), 0.0), axis=0, keepdims=True)
        logs.append(peak + jnp.log2(total))
    src = src_ref[...]
    norm = jnp.full((PARTS, 128), DEAD, f32)
    for h, log in enumerate(logs):
        got = jnp.take_along_axis(jnp.broadcast_to(log, (PARTS, 128)), jnp.bitwise_and(src, 127), axis=1)
        norm = jnp.where((src >= h * 128) & (src < (h + 1) * 128), got, norm)
    log_sum = LN2 * jnp.sum(sum(logs), axis=1, keepdims=True) - local_sq / (sharpness * mean)
    spare = jnp.bitwise_and(quarter + CAP, 127)
    return jnp.where(iota((PARTS, 128), 1) == spare, log_sum, norm)


def sum_logs(dp, cent, norm):
    lane = iota((PARTS, 128), 1)
    j = jnp.bitwise_and(iota((PARTS, 128), 0) * STRIDE, PARTS - 1)
    outer = jnp.bitwise_and(dp + OUTER - jnp.right_shift(j, 4), OUTER - 1)
    sender = outer * INNER + jnp.bitwise_and(cent + PARTS - j, INNER - 1)
    quarter = jnp.bitwise_and(iota((PARTS, 128), 0), 3) * CAP
    spare = jnp.bitwise_and(quarter + CAP, 127)
    log_sum = jnp.sum(jnp.where(lane == spare, norm, 0.0), axis=1, keepdims=True)
    log_sum = jnp.sum(jnp.where(lane == sender, log_sum, 0.0), axis=0, keepdims=True)
    log_sum = jnp.sum(log_sum, axis=1, keepdims=True)
    return log_sum


def unpack_norms(norm_in_ref, norms_ref, peak_ref, half):
    count = PARTS // 2
    norm = norm_in_ref[half * count : (half + 1) * count].reshape(count, 128)
    quarter = jnp.bitwise_and(iota((count, 128), 0), 3) * CAP
    mine = jnp.where(jnp.bitwise_and(iota((count, 128), 1), 96) == quarter, norm, 0.0)
    norms_ref[half * count // 4 : (half + 1) * count // 4, :] = jnp.sum(mine.reshape(count // 4, 4, 128), axis=1)
    for t in range(half * GROUPS // 2, (half + 1) * GROUPS // 2):
        norm = jnp.concatenate([norms_ref[2 * t : 2 * t + 1, :], norms_ref[2 * t + 1 : 2 * t + 2, :]], axis=1)
        peak_ref[t] = jnp.exp2(peak_ref[t] - norm)


def kernel(
    owners_ref, vectors_ref, centroids_ref, penalty_ref, out_ref, energy_ref,
    send_ref, x_ref, u_ref, bias_ref, rank_ref, src_ref,
    sq_ref, outer_ref, inner_ref, lse_ref, lse_in_ref, norm_ref, norm_in_ref, norms_ref, mass_ref, peak_ref,
    x_out, x_in, sq_out, sq_in, lse_out, lse_in, norm_out, norm_in,
):
    dp, cent = lax.axis_index("dp"), lax.axis_index("cent")
    n, d = centroids_ref.shape
    rows = vectors_ref.shape[0]
    barrier = pltpu.get_barrier_semaphore()

    def greet(g):
        for i in range(g * GROUP, (g + 1) * GROUP):
            if i > 0:
                pl.semaphore_signal(barrier, inc=1, device_id=ahead(dp, cent, i), device_id_type=LOGICAL)

    arrange(greet, dp, cent, owners_ref[...], vectors_ref, send_ref, rank_ref, src_ref)
    x_ref[0] = send_ref[0]
    v = vectors_ref[...].astype(f32)
    local_sq = jnp.sum(jnp.sum(v * v, axis=0, keepdims=True), axis=1, keepdims=True)
    sq_ref[0] = jnp.broadcast_to(local_sq, (1, 128))
    outer_ref[0] = sq_ref[0]
    pl.semaphore_wait(barrier, PARTS - 1)

    def copy(src, dst, out_sem, in_sem, device):
        return pltpu.make_async_remote_copy(
            src_ref=src, dst_ref=dst, send_sem=out_sem, recv_sem=in_sem, device_id=device, device_id_type=LOGICAL
        )

    def wait_bytes(ref, sem):
        pltpu.make_async_copy(ref, ref, sem).wait()

    for i in range(1, OUTER):
        device = lax.rem(dp + i, OUTER) * INNER + cent
        copy(sq_ref.at[0], outer_ref.at[i], sq_out.at[0], sq_in.at[0], device).start()

    def send_group(g):
        for k in range(GROUP):
            i = g * GROUP + k
            if isinstance(g, int) and i == 0:
                continue
            copy(send_ref.at[i], x_ref.at[i], x_out.at[g], x_in.at[g], ahead(dp, cent, i)).start()

    for g in range(AHEAD):
        send_group(g)
    wait_bytes(outer_ref.at[pl.ds(1, OUTER - 1)], sq_in.at[0])
    sq_ref[1] = jnp.sum(outer_ref[...], axis=0)
    inner_ref[0] = sq_ref[1]
    for i in range(1, INNER):
        device = dp * INNER + lax.rem(cent + i, INNER)
        copy(sq_ref.at[1], inner_ref.at[i], sq_out.at[1], sq_in.at[1], device).start()
    invert_ranks(rank_ref, src_ref)
    wait_bytes(inner_ref.at[pl.ds(1, INNER - 1)], sq_in.at[1])
    mean = jnp.sum(inner_ref[...], axis=0) * (1.0 / (rows * PARTS * d))
    fill_bias(mean, centroids_ref, penalty_ref, bias_ref)
    factor = LOG2E * 2.0 / (sharpness * mean)
    factor = jnp.concatenate([factor, factor], axis=1)

    def send_lse(t):
        for k in range(GROUP):
            i = t * GROUP + k
            if isinstance(t, int) and i == 0:
                continue
            copy(lse_ref.at[t * 2 + k // 4], lse_in_ref.at[i], lse_out, lse_in, behind(dp, cent, i)).start()

    def chunk(t):
        x = x_ref[pl.ds(t * GROUP, GROUP)].reshape(GROUP * CAP, d)
        peak, lse = chunk_stats(factor, x, t, centroids_ref, bias_ref, u_ref, 256)
        peak_ref[t] = peak
        lse_ref[2 * t] = lse[:, :128]
        lse_ref[2 * t + 1] = lse[:, 128:]

    wait_bytes(x_ref.at[pl.ds(1, GROUP - 1)], x_out.at[0])
    send_group(AHEAD)
    wait_bytes(x_ref.at[pl.ds(1, GROUP - 1)], x_in.at[0])
    chunk(0)
    lse_in_ref[0] = lse_ref[0]
    send_lse(0)

    def later(t, _):
        group = x_ref.at[pl.ds(t * GROUP, GROUP)]
        wait_bytes(group, x_out.at[t])

        @pl.when(t < GROUPS - AHEAD)
        def _():
            send_group(t + AHEAD)

        wait_bytes(group, x_in.at[t])
        chunk(t)
        send_lse(t)
        return 0

    lax.fori_loop(1, GROUPS, later, 0)
    wait_bytes(lse_in_ref.at[pl.ds(1, PARTS - 1)], lse_in)
    norm = home(mean[:, 0:1], local_sq, lse_in_ref[...].reshape(PARTS, 128), rank_ref, src_ref)
    norm_ref[...] = norm.reshape(norm_ref.shape)
    norm_in_ref[0] = norm_ref[0]

    def send_norm(half):
        def one(i, _):
            copy(norm_ref.at[i], norm_in_ref.at[i], norm_out, norm_in.at[half], ahead(dp, cent, i)).start()
            return 0

        return one

    lax.fori_loop(1, PARTS // 2, send_norm(0), 0, unroll=True)
    lax.fori_loop(PARTS // 2, PARTS, send_norm(1), 0, unroll=True)
    kb = 256

    def block(half):
        def run(b, _):
            ks = pl.ds(pl.multiple_of(b * kb, kb), kb)
            acc = jnp.zeros((kb, d), f32)
            mass = jnp.zeros((kb, 128), f32)
            for t in range(half * GROUPS // 2, (half + 1) * GROUPS // 2):
                x = x_ref[t * GROUP : (t + 1) * GROUP].reshape(GROUP * CAP, d)
                w = (u_ref[t, ks, :] * peak_ref[t]).astype(bf16)
                acc = acc + jnp.dot(w, x, preferred_element_type=f32)
                w = w.astype(f32)
                mass = mass + w[:, :128] + w[:, 128:]
            if half == 0:
                out_ref[ks, :] = acc
                mass_ref[ks, :] = mass
            else:
                mass = jnp.sum(mass + mass_ref[ks, :], axis=1, keepdims=True)
                out_ref[ks, :] = (centroids_ref[ks, :].astype(f32) + (acc + out_ref[ks, :])) / (1.0 + mass)
            return 0

        return run

    wait_bytes(norm_in_ref.at[pl.ds(1, PARTS // 2 - 1)], norm_in.at[0])
    unpack_norms(norm_in_ref, norms_ref, peak_ref, 0)
    lax.fori_loop(0, n // kb, block(0), 0)
    wait_bytes(norm_in_ref.at[pl.ds(PARTS // 2, PARTS // 2)], norm_in.at[1])
    unpack_norms(norm_in_ref, norms_ref, peak_ref, 1)
    log_sum = sum_logs(dp, cent, norm_in_ref[...].reshape(PARTS, 128))
    energy_ref[...] = jnp.broadcast_to(log_sum * (-1.0 / (energy_scale * rows * PARTS)), energy_ref.shape)
    lax.fori_loop(0, n // kb, block(1), 0)
    wait_bytes(outer_ref.at[pl.ds(1, OUTER - 1)], sq_out.at[0])
    wait_bytes(inner_ref.at[pl.ds(1, INNER - 1)], sq_out.at[1])
    wait_bytes(lse_in_ref.at[pl.ds(1, PARTS - 1)], lse_out)
    wait_bytes(norm_in_ref.at[pl.ds(1, PARTS - 1)], norm_out)


def body(vectors, owners, centroids, penalty):
    rows, d = vectors.shape
    n = centroids.shape[0]
    shape = jax.ShapeDtypeStruct
    dma = pltpu.SemaphoreType.DMA
    line = (1, 128)
    refined, energy = pl.pallas_call(
        kernel,
        out_shape=(pltpu.VMEM((n, d), f32), shape(line, f32)),
        scratch_shapes=[
            pltpu.VMEM((PARTS, CAP, d), bf16),
            pltpu.VMEM((PARTS, CAP, d), bf16),
            pltpu.VMEM((PARTS // GROUP, n, GROUP * CAP), f32),
            pltpu.VMEM((n, 128), f32),
            pltpu.VMEM((PARTS, rows), i32),
            pltpu.VMEM((PARTS, 128), i32),
            pltpu.VMEM((2,) + line, f32),
            pltpu.VMEM((OUTER,) + line, f32),
            pltpu.VMEM((INNER,) + line, f32),
            pltpu.VMEM((PARTS // 4,) + line, f32),
            pltpu.VMEM((PARTS,) + line, f32),
            pltpu.VMEM((PARTS,) + line, f32),
            pltpu.VMEM((PARTS,) + line, f32),
            pltpu.VMEM((PARTS // 4, 128), f32),
            pltpu.VMEM((n, 128), f32),
            pltpu.VMEM((GROUPS, 1, GROUP * CAP), f32),
            dma((GROUPS,)),
            dma((GROUPS,)),
            dma((2,)),
            dma((2,)),
            dma,
            dma,
            dma,
            dma((2,)),
        ],
        compiler_params=pltpu.CompilerParams(
            collective_id=0, has_side_effects=True, vmem_limit_bytes=48 * MIB
        ),
    )(owners.T, vectors, centroids, penalty.reshape(n // 128, 128))
    return refined, energy[0, 0]


def solution(mesh):
    placed = (P(AXES, None), P(AXES, None), P(AXES, None), P(AXES))
    return jax.shard_map(
        body, mesh=mesh, in_specs=placed, out_specs=(P(AXES, None), P()), check_vma=False
    )
```
